256 devices in a mesh: rows: 16 (over x, y), cols: 16 (over z, core).
Axes of the slice: x: 4, y: 4, z: 8, core: 2. Of those that a mesh axis runs over, the one named last changes fastest.
Arguments:
- weight: float32 [12288, 16384], P(('rows', 'cols')), may hold values from -6 to 6
- factor_panel: float32 [2, 16, 512, 1024], P(None, 'cols'), may hold values from -0.1875 to 0.1875
- diag_inverse: float32 [2, 512, 512], P(None, 'rows'), may hold values from -2 to 2, as said below
Outputs:
- whitened: float32 [12288, 2, 16, 512], P('rows', None, 'cols')
The draws below stay inside these ranges and needn't reach their ends.
Inputs may be any that keep to these rules, and one draw needn't show every extreme that they name: `diag_inverse`: each of the two blocks is lower triangular with diagonal entries between 0.5 and 2.
All inputs are finite; a program needn't handle non-finite values.
Results may differ from the reference program's by a relative error of at most 0.00007.
Values sent between devices are 32-bit elements; how exact they have to be, the bound alone decides.
No kernel may reach another device: no remote copies, remote signals or barrier semaphores. Data moves between devices by JAX's collectives and lax.ppermute only.
A program may use at most 64 MiB of HBM per device.

```python
import math
import jax
import jax.numpy as jnp
from jax import lax

D = 16384
BLOCK = 512
R = 12288
CYC = 2
N_COLS = 16


def draw_diag_inverse(key, part):
    first_key, second_key = jax.random.split(jax.random.fold_in(key, 7))
    spread = jax.random.normal(first_key, (2, BLOCK, BLOCK), jnp.float32)
    spread = jnp.clip(spread, -6.0, 6.0) / math.sqrt(BLOCK)
    diagonal = jnp.exp(jax.random.uniform(second_key, (2, BLOCK), jnp.float32, math.log(0.5), math.log(2.0)))
    identity = jnp.eye(BLOCK, dtype=jnp.float32)
    return jnp.tril(spread, -1) + diagonal[:, :, None] * identity[None]


def shard_levels(stream_key, dims, cuts, smallest, high):
    loudness = 1.0
    for position, parts in cuts:
        steps = jax.random.uniform(jax.random.fold_in(jax.random.fold_in(stream_key, 6), position), (parts,), jnp.float32, smallest / len(cuts), high / len(cuts))
        loudness = loudness * jnp.repeat(jnp.exp(steps), dims[position] // parts).reshape((-1,) + (1,) * (len(dims) - 1 - position))
    return loudness


def noise(rng, shape, deviation, most, shards=(), kind=jnp.bfloat16):
    factor_of = shard_levels(rng, shape, shards, -0.22, 0.18) if shards else 1.0
    result = jax.random.normal(rng, shape, jnp.float32) * deviation * factor_of
    return jnp.minimum(jnp.maximum(result, -most), most).astype(kind)


def setup_inputs(seed: int = 0) -> dict:
    key_list = jax.random.split(jax.random.key(seed), 4)
    weight = noise(key_list[0], (R, D), 1.0, 6.0, ((0, 256),), jnp.float32)
    factor_panel = noise(key_list[1], (CYC, N_COLS, BLOCK, 2 * BLOCK), (2 * BLOCK) ** -0.5, 0.1875, ((1, 16),), jnp.float32)
    diag_inverse = draw_diag_inverse(jax.random.fold_in(key_list[3], 71), 0)
    return dict(weight=weight, factor_panel=factor_panel, diag_inverse=diag_inverse)


def reference(weight, factor_panel, diag_inverse):
    high = lax.Precision.HIGHEST
    blocks = weight.reshape(R, CYC * N_COLS, BLOCK)
    panel = factor_panel.reshape(CYC * N_COLS, BLOCK, 2 * BLOCK)
    solved_first = jnp.dot(blocks[:, 0], diag_inverse[0].T, precision=high)
    updated = blocks - jnp.einsum("rk,jik->rji", solved_first, panel[:, :, :BLOCK], precision=high)
    solved_second = jnp.dot(updated[:, 1], diag_inverse[1].T, precision=high)
    updated = updated - jnp.einsum("rk,jik->rji", solved_second, panel[:, :, BLOCK:], precision=high)
    updated = updated.at[:, 0].set(solved_first).at[:, 1].set(solved_second)
    return updated.reshape(R, CYC, N_COLS, BLOCK)
```

```python
import functools

import jax
import jax.numpy as jnp
from jax import lax
from jax.experimental import pallas as pl
from jax.experimental.pallas import tpu as pltpu
from jax.sharding import PartitionSpec as P

B = 512
CHUNKS = ((0, 8), (8, 8), (16, 8), (24, 24))
NT = (((1,), (1,)), ((), ()))
VMEM = pltpu.CompilerParams(vmem_limit_bytes=40 << 20)
SIDE = 4


def dot_exact(left, right):
    return lax.dot_general(left, right, NT, precision=lax.Precision.HIGHEST, preferred_element_type=jnp.float32)


def dot_half(left, right):
    return lax.dot_general(left, right, NT, preferred_element_type=jnp.float32)


def split(value):
    high = value.astype(jnp.bfloat16)
    return high, (value - high.astype(jnp.float32)).astype(jnp.bfloat16)


def pack_body(rows, w_ref, o_ref):
    for c in range(16):
        for h in range(2):
            for k in range(4):
                o_ref[c, h * 4 + k] = w_ref[:, pl.ds((h * 16 + c) * B + k * 128, 128)]


def pack(weight, first, rows):
    return pl.pallas_call(
        functools.partial(pack_body, rows),
        grid=(1,),
        out_shape=jax.ShapeDtypeStruct((16, 8, rows, 128), jnp.float32),
        in_specs=[pl.BlockSpec((rows, weight.shape[1]), lambda i: (first // rows, 0))],
        out_specs=pl.BlockSpec((16, 8, rows, 128), lambda i: (0, 0, 0, 0)),
        compiler_params=VMEM,
        cost_estimate=pl.CostEstimate(flops=0, bytes_accessed=2 * rows * 65536, transcendentals=0),
    )(weight)


def solve_body(own_ref, other_ref, *refs):
    blocks, (x_ref, w_scr, d0_scr, d1_scr, l_scr) = refs[:9], refs[9:]
    r, c = lax.axis_index("rows"), lax.axis_index("cols")
    x, y, z, parity = r // 4, r % 4, c // 2, c % 2
    for q in range(16):
        dx, dy = (q // 4 - x + 4) % 4, (q % 4 - y + 4) % 4
        at_even, at_odd = dx * 4 + dy, dy * 4 + dx
        own = own_ref[jnp.where(parity == 0, at_even, at_odd)]
        other = other_ref[jnp.where(parity == 0, at_odd, at_even)]
        even = jnp.where(parity == 0, own, other)
        odd = jnp.where(parity == 0, other, own)
        d0_scr[32 * q : 32 * q + 32] = even[:32]
        l_scr[32 * q : 32 * q + 32] = odd[:32]
        d1_scr[32 * q : 32 * q + 16] = even[32:]
        d1_scr[32 * q + 16 : 32 * q + 32] = odd[32:]
    for i in range(7):
        w_scr[48 * i : 48 * i + 48] = blocks[i][...]
    w_scr[336:360] = blocks[7][...]
    w_scr[360:384] = blocks[8][...]
    first = dot_exact(w_scr[:, :B], d0_scr[...])
    second = dot_exact(w_scr[:, B:] - dot_exact(first, l_scr[...]), d1_scr[...])
    for i, shift in enumerate((0, 7, 1, 6, 2, 5, 3, 4)):
        at = (z + shift) % 8
        x_ref[at, :, :B] = first[48 * i : 48 * i + 48]
        x_ref[at, :, B:] = second[48 * i : 48 * i + 48]


def solve(own, other, blocks):
    return pl.pallas_call(
        solve_body,
        out_shape=jax.ShapeDtypeStruct((8, 48, 2 * B), jnp.float32),
        scratch_shapes=[
            pltpu.VMEM((384, 2 * B), jnp.float32),
            pltpu.VMEM((B, B), jnp.float32),
            pltpu.VMEM((B, B), jnp.float32),
            pltpu.VMEM((B, B), jnp.float32),
        ],
        compiler_params=VMEM,
        cost_estimate=pl.CostEstimate(flops=6 * 6 * 384 * B * B, bytes_accessed=6 << 20, transcendentals=0),
    )(own, other, *blocks)


def product_body(own_ref, other_ref, panel_ref, p_ref, xh_scr, xl_scr):
    c = lax.axis_index("cols")
    parity = c % 2
    for part, ref in ((parity, own_ref), (1 - parity, other_ref)):
        for z in range(8):
            value = ref[z]
            high, low = split(value)
            at = pl.multiple_of((2 * z + part) * 48, 16)
            xh_scr[pl.ds(at, 48)] = high
            xl_scr[pl.ds(at, 48)] = low

    def step(j, carry):
        h, i = j // 2, j % 2
        lh, ll = split(panel_ref[h, 0, pl.ds(pl.multiple_of(i * 256, 256), 256), :])
        out = dot_half(xh_scr[...], lh) + (dot_half(xl_scr[...], lh) + dot_half(xh_scr[...], ll))
        p_ref[:, :, pl.ds(pl.multiple_of(j * 256, 256), 256)] = out.reshape(16, 48, 256)
        return carry

    lax.fori_loop(0, 4, step, 0)

    for which in range(2):

        @pl.when(c == which)
        def _():
            for part, ref in ((parity, own_ref), (1 - parity, other_ref)):
                for z in range(8):
                    p_ref[2 * z + part, :, :B] = -ref[z, :, which * B : which * B + B]


def product(own, other, panel):
    return pl.pallas_call(
        product_body,
        out_shape=jax.ShapeDtypeStruct((16, 48, 2 * B), jnp.float32),
        scratch_shapes=[pltpu.VMEM((768, 2 * B), jnp.bfloat16), pltpu.VMEM((768, 2 * B), jnp.bfloat16)],
        compiler_params=VMEM,
        cost_estimate=pl.CostEstimate(flops=2 * 3 * 768 * 1024 * 1024, bytes_accessed=10 << 20, transcendentals=0),
    )(own, other, panel)


def finish_body(rows, w_ref, p_ref, *rest):
    o_ref = rest[-1]
    solved = lax.axis_index("cols") < 2
    for s in range(16):
        for k in range(8):
            w = w_ref[s, k]
            if k < 4:
                w = jnp.where(solved, jnp.zeros_like(w), w)
            o_ref[s, pl.ds(k, rows, stride=8), :] = w - p_ref[s, :, k * 128 : k * 128 + 128]


def finish(part, prod, out, first, rows):
    at = first // rows
    extra = [] if out is None else [out]
    return pl.pallas_call(
        functools.partial(finish_body, rows),
        grid=(1,),
        out_shape=jax.ShapeDtypeStruct((16, 384, 128), jnp.float32),
        in_specs=[
            pl.BlockSpec((16, 8, rows, 128), lambda i: (0, 0, 0, 0)),
            pl.BlockSpec((16, rows, 2 * B), lambda i: (0, at, 0)),
        ]
        + [pl.BlockSpec(memory_space=pl.ANY)] * len(extra),
        out_specs=pl.BlockSpec((16, rows * 8, 128), lambda i: (0, at, 0)),
        input_output_aliases={} if out is None else {2: 0},
        compiler_params=VMEM,
        cost_estimate=pl.CostEstimate(flops=rows * 16384, bytes_accessed=3 * rows * 65536, transcendentals=0),
    )(part, prod, *extra)


def plane_shift(amount, first_phase):
    pairs = []
    for x in range(SIDE):
        for y in range(SIDE):
            for c in range(16):
                along_y = first_phase == (c % 2 == 0)
                tx, ty = (x, (y + amount) % SIDE) if along_y else ((x + amount) % SIDE, y)
                pairs.append(((x * SIDE + y) * 16 + c, (tx * SIDE + ty) * 16 + c))
    return pairs


UP = [(i, (i + 2) % 16) for i in range(16)]
DOWN = [(i, (i - 2) % 16) for i in range(16)]
TWIN = [(i, i ^ 1) for i in range(16)]


def along(value, pairs):
    return lax.ppermute(value, "cols", pairs)


def plane_gather(value):
    for phase in (True, False):
        got = [lax.ppermute(value, ("rows", "cols"), plane_shift(a, phase)) for a in (-1, 2, 1)]
        value = jnp.stack([value] + got)
    return value.reshape((16,) + value.shape[2:])


def exchange(part):
    return lax.all_to_all(part, "cols", split_axis=0, concat_axis=0, tiled=True)


def per_device(weight, factor_panel, diag_inverse):
    r, c = lax.axis_index("rows"), lax.axis_index("cols")
    even = c % 2 == 0

    lead = weight[:, : 2 * B]
    slab = lax.dynamic_slice(factor_panel, (0, 0, r * 32, 0), (1, 1, 32, B))[0, 0]
    far = along(slab, [(1, 5)]) + along(slab, [(1, 13)])
    slab = jnp.where(c == 1, slab, far)
    near = along(slab, [(1, 3), (5, 7), (13, 11)]) + along(slab, [(1, 15), (5, 9)])
    slab = jnp.where((c == 1) | (c == 5) | (c == 13), slab, near)

    half = jnp.concatenate(
        [
            jnp.where(even, diag_inverse[0], slab),
            jnp.where(even, diag_inverse[1, :16], diag_inverse[1, 16:]),
        ]
    )
    own = plane_gather(half)
    other = along(own, TWIN)

    blocks = [lead]
    up, down = lead, lead
    parts = []
    for step, (first, rows) in enumerate(CHUNKS):
        if step == 3:
            up, down = up[:24], down[24:]
        up, down = along(up, UP), along(down, DOWN)
        weight, up, down = lax.optimization_barrier((weight, up, down))
        blocks += [up, down]
        parts.append(exchange(pack(weight, first, rows)))

    mine = solve(own, other, blocks)
    theirs = along(mine, TWIN)
    prod = product(mine, theirs, factor_panel)
    out = None
    for part, (first, rows) in zip(parts, CHUNKS):
        out = finish(part, prod, out, first, rows)
    return out.reshape(768, 2, 1, B)


def solution(mesh):
    placed = (P(("rows", "cols"), None), P(None, "cols", None, None), P(None, "rows", None))
    return jax.shard_map(
        per_device,
        mesh=mesh,
        in_specs=placed,
        out_specs=P("rows", None, "cols", None),
        check_vma=False,
    )
```

```python
import functools

import jax
import jax.numpy as jnp
from jax import lax
from jax.experimental import pallas as pl
from jax.experimental.pallas import tpu as pltpu
from jax.sharding import PartitionSpec as P

B = 512
NT = (((1,), (1,)), ((), ()))
SIDE = 4
COST = pl.CostEstimate(flops=1024, bytes_accessed=1024, transcendentals=0)


def dot_exact(left, right):
    return lax.dot_general(left, right, NT, precision=lax.Precision.HIGHEST, preferred_element_type=jnp.float32)


def dot_half(left, right):
    return lax.dot_general(left, right, NT, preferred_element_type=jnp.float32)


def split(value):
    high = value.astype(jnp.bfloat16)
    return high, (value - high.astype(jnp.float32)).astype(jnp.bfloat16)


def pack_body(w_ref, o_ref):
    for c in range(16):
        for k in range(8):
            o_ref[c, k] = w_ref[:, pl.ds(((k // 4) * 16 + c) * B + (k % 4) * 128, 128)]


def pack(weight):
    return pl.pallas_call(
        pack_body,
        out_shape=jax.ShapeDtypeStruct((16, 8, 48, 128), jnp.float32),
        compiler_params=pltpu.CompilerParams(vmem_limit_bytes=8 << 20),
        cost_estimate=COST,
    )(weight)


def choose_body(slab_ref, inverse_ref, o_ref):
    even = lax.axis_index("cols") % 2 == 0
    o_ref[:32] = jnp.where(even, inverse_ref[0], slab_ref[...])
    o_ref[32:] = jnp.where(even, inverse_ref[1, :16], inverse_ref[1, 16:])


def choose(slab, inverse):
    return pl.pallas_call(
        choose_body,
        out_shape=jax.ShapeDtypeStruct((48, B), jnp.float32),
        compiler_params=pltpu.CompilerParams(vmem_limit_bytes=4 << 20),
        cost_estimate=pl.CostEstimate(flops=10**12, bytes_accessed=10**9, transcendentals=0),
    )(slab, inverse)


def solve_body(own_ref, other_ref, *refs):
    blocks, (x_ref, w_scr, d0_scr, d1_scr, l_scr) = refs[:9], refs[9:]
    r, c = lax.axis_index("rows"), lax.axis_index("cols")
    x, y, z, parity = r // 4, r % 4, c // 2, c % 2
    for q in range(16):
        dx, dy = (q // 4 - x + 4) % 4, (q % 4 - y + 4) % 4
        at_even, at_odd = dx * 4 + dy, dy * 4 + dx
        own = own_ref[jnp.where(parity == 0, at_even, at_odd)]
        other = other_ref[jnp.where(parity == 0, at_odd, at_even)]
        even = jnp.where(parity == 0, own, other)
        odd = jnp.where(parity == 0, other, own)
        d0_scr[32 * q : 32 * q + 32] = even[:32]
        l_scr[32 * q : 32 * q + 32] = odd[:32]
        d1_scr[32 * q : 32 * q + 16] = even[32:]
        d1_scr[32 * q + 16 : 32 * q + 32] = odd[32:]
    for i in range(7):
        w_scr[48 * i : 48 * i + 48] = blocks[i][...]
    w_scr[336:360] = blocks[7][...]
    w_scr[360:384] = blocks[8][...]
    first = dot_exact(w_scr[:, :B], d0_scr[...])
    second = dot_exact(w_scr[:, B:] - dot_exact(first, l_scr[...]), d1_scr[...])
    for i, shift in enumerate((0, 7, 1, 6, 2, 5, 3, 4)):
        at = (z + shift) % 8
        x_ref[at, :, :B] = first[48 * i : 48 * i + 48]
        x_ref[at, :, B:] = second[48 * i : 48 * i + 48]


def solve(own, other, blocks):
    return pl.pallas_call(
        solve_body,
        out_shape=jax.ShapeDtypeStruct((8, 48, 2 * B), jnp.float32),
        scratch_shapes=[
            pltpu.VMEM((384, 2 * B), jnp.float32),
            pltpu.VMEM((B, B), jnp.float32),
            pltpu.VMEM((B, B), jnp.float32),
            pltpu.VMEM((B, B), jnp.float32),
        ],
        compiler_params=pltpu.CompilerParams(vmem_limit_bytes=20 << 20),
        cost_estimate=COST,
    )(own, other, *blocks)


def product_body(own_ref, other_ref, panel_ref, out_ref, xh_scr, xl_scr, p_ref):
    c = lax.axis_index("cols")
    parity = c % 2
    for part, ref in ((parity, own_ref), (1 - parity, other_ref)):
        for z in range(8):
            value = ref[z]
            high, low = split(value)
            at = pl.multiple_of((2 * z + part) * 48, 16)
            xh_scr[pl.ds(at, 48)] = high
            xl_scr[pl.ds(at, 48)] = low

    def step(j, carry):
        h, i = j // 2, j % 2
        lh, ll = split(panel_ref[h, 0, pl.ds(pl.multiple_of(i * 256, 256), 256), :])
        out = dot_half(xh_scr[...], lh) + (dot_half(xl_scr[...], lh) + dot_half(xh_scr[...], ll))
        p_ref[:, :, pl.ds(pl.multiple_of(j * 256, 256), 256)] = out.reshape(16, 48, 256)
        return carry

    lax.fori_loop(0, 4, step, 0)

    for which in range(2):

        @pl.when(c == which)
        def _():
            for part, ref in ((parity, own_ref), (1 - parity, other_ref)):
                for z in range(8):
                    p_ref[2 * z + part, :, :B] = -ref[z, :, which * B : which * B + B]

    pltpu.sync_copy(p_ref, out_ref)


def product(own, other, panel):
    return pl.pallas_call(
        product_body,
        out_shape=jax.ShapeDtypeStruct((16, 48, 2 * B), jnp.float32),
        out_specs=pl.BlockSpec(memory_space=pltpu.HBM),
        scratch_shapes=[
            pltpu.VMEM((768, 2 * B), jnp.bfloat16),
            pltpu.VMEM((768, 2 * B), jnp.bfloat16),
            pltpu.VMEM((16, 48, 2 * B), jnp.float32),
        ],
        compiler_params=pltpu.CompilerParams(vmem_limit_bytes=24 << 20),
        cost_estimate=COST,
    )(own, other, panel)


def finish_body(w_ref, prod_ref, o_ref, p_scr, scr, in_sems, out_sems):
    solved = lax.axis_index("cols") < 2
    reads = [pltpu.make_async_copy(prod_ref.at[s], p_scr.at[s], in_sems.at[s]) for s in range(16)]
    writes = [pltpu.make_async_copy(scr.at[s], o_ref.at[s], out_sems.at[s]) for s in range(16)]
    for read in reads:
        read.start()
    for s in range(16):
        reads[s].wait()
        for k in range(8):
            w = w_ref[s, k]
            if k < 4:
                w = jnp.where(solved, jnp.zeros_like(w), w)
            scr[s, pl.ds(k, 48, stride=8), :] = w - p_scr[s, :, k * 128 : k * 128 + 128]
        writes[s].start()
    for write in writes:
        write.wait()


def finish(part, prod):
    return pl.pallas_call(
        finish_body,
        out_shape=jax.ShapeDtypeStruct((16, 384, 128), jnp.float32),
        in_specs=[pl.BlockSpec(memory_space=pltpu.VMEM), pl.BlockSpec(memory_space=pltpu.HBM)],
        out_specs=pl.BlockSpec(memory_space=pltpu.HBM),
        scratch_shapes=[
            pltpu.VMEM((16, 48, 2 * B), jnp.float32),
            pltpu.VMEM((16, 384, 128), jnp.float32),
            pltpu.SemaphoreType.DMA((16,)),
            pltpu.SemaphoreType.DMA((16,)),
        ],
        compiler_params=pltpu.CompilerParams(vmem_limit_bytes=16 << 20),
        cost_estimate=COST,
    )(part, prod)


def plane_shift(amount, first_phase):
    pairs = []
    for x in range(SIDE):
        for y in range(SIDE):
            for c in range(16):
                along_y = first_phase == (c % 2 == 0)
                tx, ty = (x, (y + amount) % SIDE) if along_y else ((x + amount) % SIDE, y)
                pairs.append(((x * SIDE + y) * 16 + c, (tx * SIDE + ty) * 16 + c))
    return pairs


UP = [(i, (i + 2) % 16) for i in range(16)]
DOWN = [(i, (i - 2) % 16) for i in range(16)]
UP2 = [(i, (i + 4) % 16) for i in range(16)]
DOWN2 = [(i, (i - 4) % 16) for i in range(16)]
TWIN = [(i, i ^ 1) for i in range(16)]


def along(value, pairs):
    return lax.ppermute(value, "cols", pairs)


def plane_step(value, phase):
    got = [lax.ppermute(value, ("rows", "cols"), plane_shift(a, phase)) for a in (-1, 2, 1)]
    return jnp.stack([value] + got)


def tie(*values):
    return lax.optimization_barrier(values)


def exchange(part):
    return lax.all_to_all(part, "cols", split_axis=0, concat_axis=0, tiled=True)


def per_device(weight, factor_panel, diag_inverse):
    r, c = lax.axis_index("rows"), lax.axis_index("cols")

    lead = weight[:, : 2 * B]
    slab = lax.dynamic_slice(factor_panel, (0, 0, r * 32, 0), (1, 1, 32, B))[0, 0]

    def hand(slab, pairs):
        targets = functools.reduce(jnp.logical_or, [c == to for _, to in pairs])
        return jnp.where(targets, along(slab, pairs), slab)

    slab = hand(hand(slab, [(1, 9)]), [(1, 5), (9, 13)])
    up2, down2 = along(lead, UP2), along(lead, DOWN2)
    up1, down1 = along(lead, UP), along(lead, DOWN)
    up2, down2, slab, packed = tie(up2, down2, slab, pack(weight))
    slab = hand(slab, [(1, 3), (5, 7), (9, 11), (13, 15)])
    up3, down3 = along(up2, UP), along(down2, DOWN)
    up4, down4 = along(up2[:24], UP2), along(down2[24:], DOWN2)
    packed, slab, up1, down1 = tie(packed, slab, up1, down1)
    part = exchange(packed)
    slab, *blocks = tie(slab, lead, up1, down1, up2, down2, up3, down3, up4, down4)
    half = choose(slab, diag_inverse)
    row = plane_step(half, True)
    own = plane_step(row, False).reshape(16, 48, B)
    other = along(own, TWIN)
    mine = solve(own, other, blocks)
    theirs = along(mine, TWIN)
    prod = product(mine, theirs, factor_panel)
    return finish(part, prod).reshape(768, 2, 1, B)


def solution(mesh):
    placed = (P(("rows", "cols"), None), P(None, "cols", None, None), P(None, "rows", None))
    return jax.shard_map(
        per_device,
        mesh=mesh,
        in_specs=placed,
        out_specs=P("rows", None, "cols", None),
        check_vma=False,
    )
```

```python
import functools

import jax
import jax.numpy as jnp
from jax import lax
from jax.experimental import pallas as pl
from jax.experimental.pallas import tpu as pltpu
from jax.sharding import PartitionSpec as P

B = 512
NT = (((1,), (1,)), ((), ()))
SIDE = 4
HEAVY = pl.CostEstimate(flops=10**12, bytes_accessed=10**9, transcendentals=0)
COST = pl.CostEstimate(flops=1024, bytes_accessed=1024, transcendentals=0)


def dot_exact(left, right):
    return lax.dot_general(left, right, NT, precision=lax.Precision.HIGHEST, preferred_element_type=jnp.float32)


def dot_half(left, right):
    return lax.dot_general(left, right, NT, preferred_element_type=jnp.float32)


def split(value):
    high = value.astype(jnp.bfloat16)
    return high, (value - high.astype(jnp.float32)).astype(jnp.bfloat16)


def pack_body(w_ref, o_ref):
    for c in range(16):
        for k in range(8):
            o_ref[c, k] = w_ref[:, pl.ds(((k // 4) * 16 + c) * B + (k % 4) * 128, 128)]


def pack(weight):
    return pl.pallas_call(
        pack_body,
        out_shape=jax.ShapeDtypeStruct((16, 8, 48, 128), jnp.float32),
        compiler_params=pltpu.CompilerParams(vmem_limit_bytes=8 << 20),
        cost_estimate=COST,
    )(weight)


def slab_body(panel_ref, o_ref):
    r = lax.axis_index("rows")
    pltpu.sync_copy(panel_ref.at[0, 0, pl.ds(pl.multiple_of(r * 32, 32), 32), pl.ds(0, B)], o_ref)


def take_slab(panel):
    return pl.pallas_call(
        slab_body,
        out_shape=jax.ShapeDtypeStruct((32, B), jnp.float32),
        in_specs=[pl.BlockSpec(memory_space=pl.ANY)],
        compiler_params=pltpu.CompilerParams(vmem_limit_bytes=4 << 20),
        cost_estimate=HEAVY,
    )(panel)


def merge_body(targets, own_ref, *refs):
    c = lax.axis_index("cols")
    value = own_ref[...]
    for to, ref in zip(targets, refs):
        value = jnp.where(c == to, ref[...], value)
    refs[-1][...] = value


def merge(own, targets, got):
    return pl.pallas_call(
        functools.partial(merge_body, targets),
        out_shape=jax.ShapeDtypeStruct(own.shape, own.dtype),
        compiler_params=pltpu.CompilerParams(vmem_limit_bytes=4 << 20),
        cost_estimate=HEAVY,
    )(own, *got)


def choose_body(slab_ref, got_ref, inverse_ref, o_ref):
    c = lax.axis_index("cols")
    even = c % 2 == 0
    slab = jnp.where(c % 4 == 1, slab_ref[...], got_ref[...])
    o_ref[:32] = jnp.where(even, inverse_ref[0], slab)
    o_ref[32:] = jnp.where(even, inverse_ref[1, :16], inverse_ref[1, 16:])


def choose(slab, got, inverse):
    return pl.pallas_call(
        choose_body,
        out_shape=jax.ShapeDtypeStruct((48, B), jnp.float32),
        compiler_params=pltpu.CompilerParams(vmem_limit_bytes=4 << 20),
        cost_estimate=HEAVY,
    )(slab, got, inverse)


def solve_body(own_ref, other_ref, *refs):
    blocks, (x_ref, w_scr, d0_scr, d1_scr, l_scr) = refs[:8], refs[8:]
    r, c = lax.axis_index("rows"), lax.axis_index("cols")
    x, y, z, parity = r // 4, r % 4, c // 2, c % 2
    for q in range(16):
        dx, dy = (q // 4 - x + 4) % 4, (q % 4 - y + 4) % 4
        at_even, at_odd = dx * 4 + dy, dy * 4 + dx
        own = own_ref[jnp.where(parity == 0, at_even, at_odd)]
        other = other_ref[jnp.where(parity == 0, at_odd, at_even)]
        even = jnp.where(parity == 0, own, other)
        odd = jnp.where(parity == 0, other, own)
        d0_scr[32 * q : 32 * q + 32] = even[:32]
        l_scr[32 * q : 32 * q + 32] = odd[:32]
        d1_scr[32 * q : 32 * q + 16] = even[32:]
        d1_scr[32 * q + 16 : 32 * q + 32] = odd[32:]
    for i in range(8):
        w_scr[48 * i : 48 * i + 48] = blocks[i][...]
    first = dot_exact(w_scr[:, :B], d0_scr[...])
    second = dot_exact(w_scr[:, B:] - dot_exact(first, l_scr[...]), d1_scr[...])
    for i, shift in enumerate((0, 7, 1, 6, 2, 5, 3, 4)):
        at = (z + shift) % 8
        x_ref[at, :, :B] = first[48 * i : 48 * i + 48]
        x_ref[at, :, B:] = second[48 * i : 48 * i + 48]


def solve(own, other, blocks):
    return pl.pallas_call(
        solve_body,
        out_shape=jax.ShapeDtypeStruct((8, 48, 2 * B), jnp.float32),
        scratch_shapes=[
            pltpu.VMEM((384, 2 * B), jnp.float32),
            pltpu.VMEM((B, B), jnp.float32),
            pltpu.VMEM((B, B), jnp.float32),
            pltpu.VMEM((B, B), jnp.float32),
        ],
        compiler_params=pltpu.CompilerParams(vmem_limit_bytes=20 << 20),
        cost_estimate=COST,
    )(own, other, *blocks)


def product_body(own_ref, other_ref, panel_ref, p_ref, xh_scr, xl_scr):
    c = lax.axis_index("cols")
    parity = c % 2
    for part, ref in ((parity, own_ref), (1 - parity, other_ref)):
        for z in range(8):
            value = ref[z]
            high, low = split(value)
            at = pl.multiple_of((2 * z + part) * 48, 16)
            xh_scr[pl.ds(at, 48)] = high
            xl_scr[pl.ds(at, 48)] = low

    def step(j, carry):
        h, i = j // 2, j % 2
        lh, ll = split(panel_ref[h, 0, pl.ds(pl.multiple_of(i * 256, 256), 256), :])
        out = dot_half(xh_scr[...], lh) + (dot_half(xl_scr[...], lh) + dot_half(xh_scr[...], ll))
        p_ref[:, :, pl.ds(pl.multiple_of(j * 256, 256), 256)] = out.reshape(16, 48, 256)
        return carry

    lax.fori_loop(0, 4, step, 0)

    for which in range(2):

        @pl.when(c == which)
        def _():
            for part, ref in ((parity, own_ref), (1 - parity, other_ref)):
                for z in range(8):
                    p_ref[2 * z + part, :, :B] = -ref[z, :, which * B : which * B + B]


def product(own, other, panel):
    return pl.pallas_call(
        product_body,
        out_shape=jax.ShapeDtypeStruct((16, 48, 2 * B), jnp.float32),
        scratch_shapes=[
            pltpu.VMEM((768, 2 * B), jnp.bfloat16),
            pltpu.VMEM((768, 2 * B), jnp.bfloat16),
        ],
        compiler_params=pltpu.CompilerParams(vmem_limit_bytes=24 << 20),
        cost_estimate=COST,
    )(own, other, panel)


def finish_body(part_ref, p_ref, o_ref, w_scr, scr, in_sems, out_sems):
    solved = lax.axis_index("cols") < 2
    reads = [pltpu.make_async_copy(part_ref.at[s], w_scr.at[s], in_sems.at[s]) for s in range(16)]
    writes = [pltpu.make_async_copy(scr.at[s], o_ref.at[s], out_sems.at[s]) for s in range(16)]
    for read in reads:
        read.start()
    for s in range(16):
        reads[s].wait()
        for k in range(8):
            w = w_scr[s, k]
            if k < 4:
                w = jnp.where(solved, jnp.zeros_like(w), w)
            scr[s, pl.ds(k, 48, stride=8), :] = w - p_ref[s, :, k * 128 : k * 128 + 128]
        writes[s].start()
    for write in writes:
        write.wait()


def finish(part, prod):
    return pl.pallas_call(
        finish_body,
        out_shape=jax.ShapeDtypeStruct((16, 384, 128), jnp.float32),
        in_specs=[pl.BlockSpec(memory_space=pl.ANY), pl.BlockSpec(memory_space=pltpu.VMEM)],
        out_specs=pl.BlockSpec(memory_space=pl.ANY),
        scratch_shapes=[
            pltpu.VMEM((16, 8, 48, 128), jnp.float32),
            pltpu.VMEM((16, 384, 128), jnp.float32),
            pltpu.SemaphoreType.DMA((16,)),
            pltpu.SemaphoreType.DMA((16,)),
        ],
        compiler_params=pltpu.CompilerParams(vmem_limit_bytes=16 << 20),
        cost_estimate=COST,
    )(part, prod)


def plane_shift(amount, first_phase):
    pairs = []
    for x in range(SIDE):
        for y in range(SIDE):
            for c in range(16):
                along_y = first_phase == (c % 2 == 0)
                tx, ty = (x, (y + amount) % SIDE) if along_y else ((x + amount) % SIDE, y)
                pairs.append(((x * SIDE + y) * 16 + c, (tx * SIDE + ty) * 16 + c))
    return pairs


UP = [(i, (i + 2) % 16) for i in range(16)]
DOWN = [(i, (i - 2) % 16) for i in range(16)]
UP2 = [(i, (i + 4) % 16) for i in range(16)]
DOWN2 = [(i, (i - 4) % 16) for i in range(16)]
SPLIT2 = [(i, (i + (4 if i % 2 == 0 else 12)) % 16) for i in range(16)]
TWIN = [(i, i ^ 1) for i in range(16)]


def along(value, pairs):
    return lax.ppermute(value, "cols", pairs)


def plane_step(value, phase):
    got = [lax.ppermute(value, ("rows", "cols"), plane_shift(a, phase)) for a in (-1, 2, 1)]
    return jnp.stack([value] + got)


def tie(*values):
    return lax.optimization_barrier(values)


def exchange(part):
    return lax.all_to_all(part, "cols", split_axis=0, concat_axis=0, tiled=True)


def per_device(weight, factor_panel, diag_inverse):
    lead = weight[:, : 2 * B]
    up1, down1 = along(lead, UP), along(lead, DOWN)
    up2, down2 = along(lead, UP2), along(lead, DOWN2)
    packed, panel = tie(pack(weight), factor_panel)
    slab = take_slab(panel)
    first, up1, down1 = tie([along(slab, [(1, to)]) for to in (5, 9, 13)], up1, down1)
    slab = merge(slab, (5, 9, 13), first)
    got = along(slab, [(1, 3), (5, 7), (9, 11), (13, 15)])
    up3, down3 = along(up2, UP), along(down2, DOWN)
    opposite = along(jnp.where(lax.axis_index("cols") % 2 == 0, up2, down2), SPLIT2)
    packed, slab = tie(packed, slab)
    part = exchange(packed)
    slab, got, *blocks = tie(slab, got, lead, up1, down1, up2, down2, up3, down3, opposite)
    half = choose(slab, got, diag_inverse)
    row = plane_step(half, True)
    own = plane_step(row, False).reshape(16, 48, B)
    other = along(own, TWIN)
    mine = solve(own, other, blocks)
    theirs = along(mine, TWIN)
    prod = product(mine, theirs, factor_panel)
    return finish(part, prod).reshape(768, 2, 1, B)


def solution(mesh):
    placed = (P(("rows", "cols"), None), P(None, "cols", None, None), P(None, "rows", None))
    return jax.shard_map(
        per_device,
        mesh=mesh,
        in_specs=placed,
        out_specs=P("rows", None, "cols", None),
        check_vma=False,
    )
```

```python
import functools

import jax
import jax.numpy as jnp
from jax import lax
from jax.experimental import pallas as pl
from jax.experimental.pallas import tpu as pltpu
from jax.sharding import PartitionSpec as P

B = 512
NT = (((1,), (1,)), ((), ()))
SIDE = 4
HEAVY = pl.CostEstimate(flops=10**12, bytes_accessed=10**9, transcendentals=0)
COST = pl.CostEstimate(flops=1024, bytes_accessed=1024, transcendentals=0)


def dot_exact(left, right):
    return lax.dot_general(left, right, NT, precision=lax.Precision.HIGHEST, preferred_element_type=jnp.float32)


def dot_half(left, right):
    return lax.dot_general(left, right, NT, preferred_element_type=jnp.float32)


def split(value):
    high = value.astype(jnp.bfloat16)
    return high, (value - high.astype(jnp.float32)).astype(jnp.bfloat16)


def pack_body(w_ref, o_ref):
    for c in range(16):
        for k in range(8):
            o_ref[c, pl.ds(k, 48, stride=8), :] = w_ref[:, pl.ds(((k // 4) * 16 + c) * B + (k % 4) * 128, 128)]


def pack(weight):
    return pl.pallas_call(
        pack_body,
        out_shape=jax.ShapeDtypeStruct((16, 384, 128), jnp.float32),
        compiler_params=pltpu.CompilerParams(vmem_limit_bytes=8 << 20),
        cost_estimate=COST,
    )(weight)


def slab_body(panel_ref, o_ref):
    r = lax.axis_index("rows")
    pltpu.sync_copy(panel_ref.at[0, 0, pl.ds(pl.multiple_of(r * 32, 32), 32), pl.ds(0, B)], o_ref)


def take_slab(panel):
    return pl.pallas_call(
        slab_body,
        out_shape=jax.ShapeDtypeStruct((32, B), jnp.float32),
        in_specs=[pl.BlockSpec(memory_space=pl.ANY)],
        compiler_params=pltpu.CompilerParams(vmem_limit_bytes=4 << 20),
        cost_estimate=HEAVY,
    )(panel)


def merge_body(targets, own_ref, *refs):
    c = lax.axis_index("cols")
    value = own_ref[...]
    for to, ref in zip(targets, refs):
        value = jnp.where(c == to, ref[...], value)
    refs[-1][...] = value


def merge(own, targets, got):
    return pl.pallas_call(
        functools.partial(merge_body, targets),
        out_shape=jax.ShapeDtypeStruct(own.shape, own.dtype),
        compiler_params=pltpu.CompilerParams(vmem_limit_bytes=4 << 20),
        cost_estimate=HEAVY,
    )(own, *got)


def choose_body(slab_ref, got_ref, inverse_ref, o_ref):
    c = lax.axis_index("cols")
    even = c % 2 == 0
    slab = jnp.where(c % 4 == 1, slab_ref[...], got_ref[...])
    o_ref[:32] = jnp.where(even, inverse_ref[0], slab)
    o_ref[32:] = jnp.where(even, inverse_ref[1, :16], inverse_ref[1, 16:])


def choose(slab, got, inverse):
    return pl.pallas_call(
        choose_body,
        out_shape=jax.ShapeDtypeStruct((48, B), jnp.float32),
        compiler_params=pltpu.CompilerParams(vmem_limit_bytes=4 << 20),
        cost_estimate=HEAVY,
    )(slab, got, inverse)


def solve_body(own_ref, other_ref, *refs):
    blocks, (x_ref, w_scr, d0_scr, d1_scr, l_scr) = refs[:8], refs[8:]
    r, c = lax.axis_index("rows"), lax.axis_index("cols")
    x, y, z, parity = r // 4, r % 4, c // 2, c % 2
    for q in range(16):
        dx, dy = (q // 4 - x + 4) % 4, (q % 4 - y + 4) % 4
        at_even, at_odd = dx * 4 + dy, dy * 4 + dx
        own = own_ref[jnp.where(parity == 0, at_even, at_odd)]
        other = other_ref[jnp.where(parity == 0, at_odd, at_even)]
        even = jnp.where(parity == 0, own, other)
        odd = jnp.where(parity == 0, other, own)
        d0_scr[32 * q : 32 * q + 32] = even[:32]
        l_scr[32 * q : 32 * q + 32] = odd[:32]
        d1_scr[32 * q : 32 * q + 16] = even[32:]
        d1_scr[32 * q + 16 : 32 * q + 32] = odd[32:]
    for i in range(8):
        w_scr[48 * i : 48 * i + 48] = blocks[i][...]
    first = dot_exact(w_scr[:, :B], d0_scr[...])
    second = dot_exact(w_scr[:, B:] - dot_exact(first, l_scr[...]), d1_scr[...])
    for i, shift in enumerate((0, 7, 1, 6, 2, 5, 3, 4)):
        at = (z + shift) % 8
        x_ref[at, :, :B] = first[48 * i : 48 * i + 48]
        x_ref[at, :, B:] = second[48 * i : 48 * i + 48]


def solve(own, other, blocks):
    return pl.pallas_call(
        solve_body,
        out_shape=jax.ShapeDtypeStruct((8, 48, 2 * B), jnp.float32),
        scratch_shapes=[
            pltpu.VMEM((384, 2 * B), jnp.float32),
            pltpu.VMEM((B, B), jnp.float32),
            pltpu.VMEM((B, B), jnp.float32),
            pltpu.VMEM((B, B), jnp.float32),
        ],
        compiler_params=pltpu.CompilerParams(vmem_limit_bytes=20 << 20),
        cost_estimate=COST,
    )(own, other, *blocks)


def product_body(own_ref, other_ref, panel_ref, p_ref, xh_scr, xl_scr):
    c = lax.axis_index("cols")
    parity = c % 2
    for part, ref in ((parity, own_ref), (1 - parity, other_ref)):
        for z in range(8):
            value = ref[z]
            high, low = split(value)
            at = pl.multiple_of((2 * z + part) * 48, 16)
            xh_scr[pl.ds(at, 48)] = high
            xl_scr[pl.ds(at, 48)] = low

    for j in range(4):
        lh, ll = split(panel_ref[j // 2, 0, j % 2 * 256 : j % 2 * 256 + 256, :])
        out = dot_half(xh_scr[...], lh) + (dot_half(xl_scr[...], lh) + dot_half(xh_scr[...], ll))
        for s in range(16):
            for t in range(2):
                p_ref[s, pl.ds(2 * j + t, 48, stride=8), :] = out[48 * s : 48 * s + 48, t * 128 : t * 128 + 128]

    for which in range(2):

        @pl.when(c == which)
        def _():
            for part, ref in ((parity, own_ref), (1 - parity, other_ref)):
                for z in range(8):
                    for k in range(4):
                        lanes = slice(which * B + k * 128, which * B + k * 128 + 128)
                        p_ref[2 * z + part, pl.ds(k, 48, stride=8), :] = -ref[z, :, lanes]


def product(own, other, panel):
    return pl.pallas_call(
        product_body,
        out_shape=jax.ShapeDtypeStruct((16, 384, 128), jnp.float32),
        scratch_shapes=[
            pltpu.VMEM((768, 2 * B), jnp.bfloat16),
            pltpu.VMEM((768, 2 * B), jnp.bfloat16),
        ],
        compiler_params=pltpu.CompilerParams(vmem_limit_bytes=24 << 20),
        cost_estimate=COST,
    )(own, other, panel)


def finish_body(part_ref, p_ref, o_ref, w_scr, scr, in_sems, out_sems):
    half = lax.broadcasted_iota(jnp.int32, (384, 128), 0) % 8
    drop = (half < 4) & (lax.axis_index("cols") < 2)
    reads = [pltpu.make_async_copy(part_ref.at[s], w_scr.at[s], in_sems.at[s]) for s in range(16)]
    writes = [pltpu.make_async_copy(scr.at[s], o_ref.at[s], out_sems.at[s]) for s in range(16)]
    for read in reads:
        read.start()
    for s in range(16):
        reads[s].wait()
        scr[s] = jnp.where(drop, 0.0, w_scr[s]) - p_ref[s]
        writes[s].start()
    for write in writes:
        write.wait()


def finish(part, prod):
    return pl.pallas_call(
        finish_body,
        out_shape=jax.ShapeDtypeStruct((16, 384, 128), jnp.float32),
        in_specs=[pl.BlockSpec(memory_space=pl.ANY), pl.BlockSpec(memory_space=pltpu.VMEM)],
        out_specs=pl.BlockSpec(memory_space=pl.ANY),
        scratch_shapes=[
            pltpu.VMEM((16, 384, 128), jnp.float32),
            pltpu.VMEM((16, 384, 128), jnp.float32),
            pltpu.SemaphoreType.DMA((16,)),
            pltpu.SemaphoreType.DMA((16,)),
        ],
        compiler_params=pltpu.CompilerParams(vmem_limit_bytes=16 << 20),
        cost_estimate=COST,
    )(part, prod)


def plane_shift(amount, first_phase):
    pairs = []
    for x in range(SIDE):
        for y in range(SIDE):
            for c in range(16):
                along_y = first_phase == (c % 2 == 0)
                tx, ty = (x, (y + amount) % SIDE) if along_y else ((x + amount) % SIDE, y)
                pairs.append(((x * SIDE + y) * 16 + c, (tx * SIDE + ty) * 16 + c))
    return pairs


UP = [(i, (i + 2) % 16) for i in range(16)]
DOWN = [(i, (i - 2) % 16) for i in range(16)]
UP2 = [(i, (i + 4) % 16) for i in range(16)]
DOWN2 = [(i, (i - 4) % 16) for i in range(16)]
SPLIT2 = [(i, (i + (4 if i % 2 == 0 else 12)) % 16) for i in range(16)]
TWIN = [(i, i ^ 1) for i in range(16)]


def along(value, pairs):
    return lax.ppermute(value, "cols", pairs)


def plane_step(value, phase):
    got = [lax.ppermute(value, ("rows", "cols"), plane_shift(a, phase)) for a in (-1, 2, 1)]
    return jnp.stack([value] + got)


def tie(*values):
    return lax.optimization_barrier(values)


def exchange(part):
    return lax.all_to_all(part, "cols", split_axis=0, concat_axis=0, tiled=True)


def per_device(weight, factor_panel, diag_inverse):
    lead = weight[:, : 2 * B]
    up1, down1 = along(lead, UP), along(lead, DOWN)
    up2, down2 = along(lead, UP2), along(lead, DOWN2)
    packed, panel = tie(pack(weight), factor_panel)
    slab = take_slab(panel)
    first, up1, down1 = tie([along(slab, [(1, to)]) for to in (5, 9, 13)], up1, down1)
    slab = merge(slab, (5, 9, 13), first)
    got = along(slab, [(1, 3), (5, 7), (9, 11), (13, 15)])
    up3, down3 = along(up2, UP), along(down2, DOWN)
    opposite = along(jnp.where(lax.axis_index("cols") % 2 == 0, up2, down2), SPLIT2)
    packed, slab = tie(packed, slab)
    part = exchange(packed)
    slab, got, *blocks = tie(slab, got, lead, up1, down1, up2, down2, up3, down3, opposite)
    half = choose(slab, got, diag_inverse)
    row = plane_step(half, True)
    own = plane_step(row, False).reshape(16, 48, B)
    other = along(own, TWIN)
    mine = solve(own, other, blocks)
    theirs = along(mine, TWIN)
    prod = product(mine, theirs, factor_panel)
    return finish(part, prod).reshape(768, 2, 1, B)


def solution(mesh):
    placed = (P(("rows", "cols"), None), P(None, "cols", None, None), P(None, "rows", None))
    return jax.shard_map(
        per_device,
        mesh=mesh,
        in_specs=placed,
        out_specs=P("rows", None, "cols", None),
        check_vma=False,
    )
```
